256 devices in a mesh: walk: 8 (over x, core), pb: 32 (over z, y).
Axes of the slice: x: 4, y: 4, z: 8, core: 2. Of those that a mesh axis runs over, the one named last changes fastest.
Arguments:
- greens: bfloat16 [128, 64, 3072], P('walk', 'pb'), may hold values from -6 to 6
- cholesky: bfloat16 [128, 300, 3072], P('pb'), may hold values from -0.011962891 to 0.011962891
- slot_source: int32 [128], replicated, may hold values from 0 to 63, as said below
- block_transfer_index: int32 [128], P('pb'), may hold values from 0 to 15
- slot_multiplicity: int32 [128], P('pb'), may hold values from 0 to 3, as said below
- fields: float32 [128, 16, 300], P('walk'), may hold values from -6 to 6
- weight: float32 [128], P('walk'), may hold values from 0.2 to 5
Outputs:
- force_bias: float32 [128, 2, 4800], P('walk', None, 'pb')
- local_energy: float32 [128], P('walk')
- new_weight: float32 [128], P('walk')
- mixed_energy: float32 [], replicated
The draws below stay inside these ranges and needn't reach their ends.
Inputs may be any that keep to these rules, and one draw needn't show every extreme that they name: `slot_source`: the Green's block of k-point k lies on index k // 2 of pb; with P = 32, slot j of pb index d (slot d * 4 + j) reads a block that lies on index (d + o_j) mod P of pb, where o_0 = 0, o_1 = P - 1, o_2 = 1, o_3 = P // 2. `slot_multiplicity`: 0 marks an empty slot; on each index of pb the live slots come first, and on some index all 4 slots are live.
All inputs are finite; a program needn't handle non-finite values.
Results may differ from the reference program's by a relative error of at most 0.0003.
Values may be sent and summed in bfloat16 or wider, within the bound.
No kernel may reach another device: no remote copies, remote signals or barrier semaphores. Data moves between devices by JAX's collectives and lax.ppermute only.
A program may use at most 320 MiB of HBM per device.

```python
import math
import jax
import jax.numpy as jnp
from jax import lax

K = 64
ORBITAL_COUNT = 96
OCCUPIED_COUNT = 16
CHOLESKY_COUNT = 300
TRANSFER_COUNT = 16
PAIR_BLOCKS_HELD = 4
NW = 128
KPOINTS_PER_PART = 2
PAIR_BLOCK_TOTAL = 128


def draw_slot_source(key, part):
    group_list = PAIR_BLOCK_TOTAL // PAIR_BLOCKS_HELD
    offsets = jnp.array([0, group_list - 1, 1, group_list // 2], dtype=jnp.int32)
    owner_parts = (jnp.arange(group_list, dtype=jnp.int32)[:, None] + offsets[None, :]) % group_list
    within_group = jax.random.randint(jax.random.fold_in(key, 12), (group_list, PAIR_BLOCKS_HELD), 0, KPOINTS_PER_PART)
    return (owner_parts * KPOINTS_PER_PART + within_group).reshape(PAIR_BLOCK_TOTAL).astype(jnp.int32)


def draw_slot_multiplicity(key, part):
    group_list = PAIR_BLOCK_TOTAL // PAIR_BLOCKS_HELD
    first_draw = jax.random.randint(jax.random.fold_in(key, 21), (group_list,), 0, PAIR_BLOCKS_HELD)
    second_draw = jax.random.randint(jax.random.fold_in(key, 22), (group_list,), 0, PAIR_BLOCKS_HELD)
    live_count = 1 + first_draw * second_draw // max(PAIR_BLOCKS_HELD - 1, 1)
    full_index = jax.random.randint(jax.random.fold_in(key, 23), (), 0, group_list)
    live_count = jnp.where(jnp.arange(group_list) == full_index, PAIR_BLOCKS_HELD, live_count)
    levels = jax.random.randint(jax.random.fold_in(key, 24), (group_list, PAIR_BLOCKS_HELD), 1, 4)
    corner = (jnp.arange(group_list)[:, None] == full_index) & (jnp.arange(PAIR_BLOCKS_HELD)[None, :] == 0)
    levels = jnp.where(corner, 3, levels)
    multiple_count = jnp.where(jnp.arange(PAIR_BLOCKS_HELD)[None, :] < live_count[:, None], levels, 0)
    return multiple_count.reshape(PAIR_BLOCK_TOTAL).astype(jnp.int32)


def touch_ends(values, rng, least, largest):
    index_at = [jax.random.randint(jax.random.fold_in(rng, axis), (), 0, length) for axis, length in enumerate(values.shape)]
    longest = values.shape.index(max(values.shape))
    neighbour = index_at[:longest] + [(index_at[longest] + 1) % values.shape[longest]] + index_at[longest + 1:]
    return values.at[tuple(index_at)].set(least).at[tuple(neighbour)].set(largest)


def block_levels(stream_key, extent, split, low, high):
    def one(dim, shards_of):
        draws = jax.random.uniform(jax.random.fold_in(jax.random.fold_in(stream_key, 6), dim), (shards_of,), jnp.float32, low / len(split), high / len(split))
        return jnp.repeat(jnp.exp(draws), extent[dim] // shards_of).reshape((-1,) + (1,) * (len(extent) - dim - 1))

    gain = one(*split[0])
    for cut in split[1:]:
        gain = gain * one(*cut)
    return gain


def bell_draw(own_key, dims, spread, bound, cuts=(), held_as=jnp.bfloat16):
    level = block_levels(own_key, dims, cuts, -0.22, 0.18) if cuts else 1.0
    entries = jax.random.normal(own_key, dims, jnp.float32) * spread * level
    return jnp.minimum(jnp.maximum(entries, -bound), bound).astype(held_as)


def setup_inputs(seed: int = 0) -> dict:
    key_list = jax.random.split(jax.random.key(seed), 8)
    greens = bell_draw(key_list[0], (NW, K, OCCUPIED_COUNT * 2 * ORBITAL_COUNT), 1.0, 6.0, ((0, 8), (1, 32)))
    cholesky = bell_draw(key_list[1], (PAIR_BLOCK_TOTAL, CHOLESKY_COUNT, OCCUPIED_COUNT * 2 * ORBITAL_COUNT), 0.002, 0.011962891, ((0, 32),))
    slot_source = draw_slot_source(jax.random.fold_in(key_list[7], 71), 0)
    block_transfer_index = touch_ends(jax.random.randint(key_list[3], (PAIR_BLOCK_TOTAL,), 0, TRANSFER_COUNT), jax.random.fold_in(key_list[3], 1), 0, TRANSFER_COUNT - 1).astype(jnp.int32)
    slot_multiplicity = draw_slot_multiplicity(jax.random.fold_in(key_list[7], 71), 0)
    fields = bell_draw(key_list[5], (NW, TRANSFER_COUNT, CHOLESKY_COUNT), 1.0, 6.0, ((0, 8),), jnp.float32)
    weight = jnp.clip(jnp.exp(math.log(5.0) - 3.218876 * jax.random.uniform(key_list[6], (NW,), jnp.float32) ** block_levels(key_list[6], (NW,), ((0, 8),), -0.2, 0.2)), 0.2, 5.0)
    return dict(greens=greens, cholesky=cholesky, slot_source=slot_source, block_transfer_index=block_transfer_index, slot_multiplicity=slot_multiplicity, fields=fields, weight=weight)


sqrt_step = 0.05

def slot_terms(chol_flat, green_flat):
    vectors = chol_flat.shape[0]
    walkers = green_flat.shape[0]
    doubled = 2 * ORBITAL_COUNT
    chol_block = chol_flat.reshape(vectors, OCCUPIED_COUNT, doubled)
    green_rows = green_flat.reshape(walkers, OCCUPIED_COUNT, doubled)
    real_part = green_rows[..., :ORBITAL_COUNT]
    imag_part = green_rows[..., ORBITAL_COUNT:]
    stacked = jnp.stack([jnp.concatenate([real_part, -imag_part], -1), jnp.concatenate([imag_part, real_part], -1)], 0)
    left_matrix = chol_block.reshape(vectors * OCCUPIED_COUNT, doubled)
    right_matrix = stacked.reshape(2 * walkers * OCCUPIED_COUNT, doubled)
    product = jnp.dot(left_matrix, right_matrix.T, preferred_element_type=jnp.float32)
    product = product.reshape(vectors, OCCUPIED_COUNT, 2, walkers, OCCUPIED_COUNT)
    identity = jnp.eye(OCCUPIED_COUNT, dtype=jnp.float32)
    diagonal = jnp.einsum('nicwj,ij->wcn', product, identity)
    crossed = jnp.einsum('nicwj,njcwi->cw', product, product)
    return (diagonal, crossed[0] - crossed[1])

def reference(greens, cholesky, slot_source, block_transfer_index, slot_multiplicity, fields, weight):

    def advance(running, inputs):
        bias, exchange_sum = running
        chol_block, source, transfer, multiple_count = inputs
        green_rows = lax.dynamic_index_in_dim(greens, source.astype(jnp.int32), 1, keepdims=False)
        diagonal, crossed = slot_terms(chol_block, green_rows)
        scaled = multiple_count.astype(jnp.float32)
        factor = scaled * (jnp.arange(TRANSFER_COUNT) == transfer).astype(jnp.float32)
        bias = bias + factor[None, None, :, None] * diagonal[:, :, None, :]
        exchange_sum = exchange_sum + scaled * crossed
        return ((bias, exchange_sum), None)
    initial = (jnp.zeros((NW, 2, TRANSFER_COUNT, CHOLESKY_COUNT), jnp.float32), jnp.zeros((NW,), jnp.float32))
    (bias, exchange_sum), unused = lax.scan(advance, initial, (cholesky, slot_source, block_transfer_index, slot_multiplicity))
    bias = bias.reshape(NW, 2, TRANSFER_COUNT * CHOLESKY_COUNT)
    real_bias = bias[:, 0]
    imag_bias = bias[:, 1]
    flat_fields = fields.reshape(NW, TRANSFER_COUNT * CHOLESKY_COUNT)
    coulomb = 0.5 * lax.optimization_barrier(jnp.sum(real_bias * real_bias - imag_bias * imag_bias, axis=1))
    energy = coulomb - 0.5 * exchange_sum
    shift_real = sqrt_step * real_bias
    shift_imag = sqrt_step * imag_bias
    real_arg = lax.optimization_barrier(jnp.sum(flat_fields * shift_real - 0.5 * (shift_real * shift_real - shift_imag * shift_imag), axis=1))
    imag_arg = lax.optimization_barrier(jnp.sum(flat_fields * shift_imag - shift_real * shift_imag, axis=1))
    new_weight = weight * jnp.exp(real_arg) * jnp.maximum(jnp.cos(imag_arg), 0.0)
    mixed = jnp.sum(weight * energy) / jnp.sum(weight)
    return (bias, energy, new_weight, mixed)
```

```python
import functools

import jax
import jax.numpy as jnp
from jax import lax
from jax.experimental import pallas as pl
from jax.experimental.pallas import tpu as pltpu
from jax.sharding import PartitionSpec as P

Q_ORB = 96
OCC = 16
CHOL = 300
TRANSFERS = 16
SLOTS = 4
DOUBLED = 2 * Q_ORB
FLAT = OCC * DOUBLED
WALKERS = 16
HALF = CHOL // 2
ROWS = 304
ROW_COUNT = 10
STEP = 0.05
F32 = jnp.float32
BF16 = jnp.bfloat16
NT = (((1,), (1,)), ((), ()))
VMEM = pl.BlockSpec(memory_space=pltpu.VMEM)


def pick_kernel(source_ref, green_ref, *out_refs):
    parts = lax.axis_size("pb")
    own = lax.axis_index("pb")
    lane = lax.broadcasted_iota(jnp.int32, (1, parts * SLOTS), 1)
    source = lax.rem(source_ref[...], 2).astype(F32)
    first = green_ref[:, 0, :].astype(F32)
    second = green_ref[:, 1, :].astype(F32)
    for j, out_ref in enumerate(out_refs):
        reader = lax.rem(own + parts - offset_of(j, parts), parts)
        kpoint = jnp.sum(jnp.where(lane == reader * SLOTS + j, source, 0.0), keepdims=True)
        out_ref[...] = jnp.where(kpoint < 0.5, first, second).astype(BF16)


def offset_of(j, parts):
    return (0, parts - 1, 1, parts // 2)[j]


def pick_call(source, greens):
    return pl.pallas_call(
        pick_kernel,
        out_shape=(jax.ShapeDtypeStruct((WALKERS, FLAT), BF16),) * SLOTS,
        in_specs=[VMEM, VMEM],
        out_specs=(VMEM,) * SLOTS,
        compiler_params=pltpu.CompilerParams(vmem_limit_bytes=4 * 2**20),
        name="pick",
    )(source, greens)


def build_right(green, right_ref):
    window = lax.broadcasted_iota(jnp.int32, (WALKERS, 256), 1)
    for c, plain in enumerate(signed_swapped(green)):
        moved = pltpu.roll(plain, 64, 1)
        for j in range(OCC):
            if j % 2 == 0:
                low = plain[:, j * DOUBLED : j * DOUBLED + 256]
                high = moved[:, j * DOUBLED : j * DOUBLED + 256]
            else:
                high = plain[:, j * DOUBLED - 64 : j * DOUBLED + 192]
                at = j * DOUBLED + 64
                if at + 256 <= FLAT:
                    low = moved[:, at : at + 256]
                else:
                    low = jnp.concatenate([moved[:, at:], moved[:, :128]], 1)
            low = jnp.where(window < DOUBLED, low, 0.0).astype(BF16)
            high = jnp.where(window >= 64, high, 0.0).astype(BF16)
            b, r = divmod(j, 4)
            for p in range(4):
                start = b * 128 + (r ^ p) * 32 + c * 16
                right_ref[p, start : start + 16, :] = low if p % 2 == 0 else high


def signed_swapped(green):
    wide = green.astype(F32)
    lane = lax.broadcasted_iota(jnp.int32, (WALKERS, FLAT), 1)
    first = lax.rem(lane, DOUBLED) < Q_ORB
    swapped = jnp.where(
        first, pltpu.roll(wide, FLAT - Q_ORB, 1), pltpu.roll(wide, Q_ORB, 1)
    )
    signed = jnp.where(first, wide, -wide)
    return signed, swapped


def diag_kernel(slots, chained, facts_ref, *refs):
    greens, rest = refs[: len(slots)], refs[len(slots) :]
    if chained:
        before_ref, chol_ref, out_ref, diag_ref = rest
        out_ref[...] = before_ref[...]
    else:
        chol_ref, out_ref, diag_ref = rest
    diag_ref[CHOL - 4 :, :] = jnp.zeros((512 - CHOL + 4, 128), F32)
    lane = lax.broadcasted_iota(jnp.int32, (16, 128), 1)
    more = HALF - 128
    spill = {}
    for at, slot in enumerate(slots):
        right = jnp.concatenate(signed_swapped(greens[at][...]), 0).astype(BF16)
        diag_ref[0:CHOL, 0:32] = lax.dot_general(
            chol_ref[slot], right, NT, preferred_element_type=F32
        )
        mult = facts_ref[0:1, slot : slot + 1]
        transfer = facts_ref[0:1, SLOTS + slot : SLOTS + slot + 1]
        for h in range(2):
            turned = jnp.transpose(diag_ref[pl.ds(h * HALF, 256), :])
            for c in range(2):
                value = mult * turned[c * 16 : c * 16 + 16, :]
                k = slot * 2 + c
                out_ref[pl.ds(h * 16 * ROW_COUNT + k, 16, stride=ROW_COUNT), :] = value[:, :128]
                tail = jnp.where(
                    lane < more, value[:, 128:], jnp.where(lane == more, transfer, 0.0)
                )
                if k % 4:
                    tail = pltpu.roll(tail, 32 * (k % 4), 1)
                key = (h, k // 4)
                spill[key] = spill[key] + tail if key in spill else tail
    for (h, block), tail in spill.items():
        rows = pl.ds(h * 16 * ROW_COUNT + 8 + block, 16, stride=ROW_COUNT)
        if chained:
            tail = tail + before_ref[rows, :]
        out_ref[rows, :] = tail


def diag_call(slots, facts, greens, before, chol):
    chained = before is not None
    return pl.pallas_call(
        functools.partial(diag_kernel, slots, chained),
        out_shape=jax.ShapeDtypeStruct((32 * ROW_COUNT, 128), F32),
        in_specs=[VMEM] * (2 + len(slots) + chained),
        out_specs=VMEM,
        scratch_shapes=[pltpu.VMEM((512, 128), F32)],
        compiler_params=pltpu.CompilerParams(vmem_limit_bytes=8 * 2**20),
        cost_estimate=pl.CostEstimate(
            flops=len(slots) * 2 * CHOL * FLAT * 256,
            bytes_accessed=len(slots) * CHOL * FLAT * 2,
            transcendentals=0,
        ),
        name="diag",
    )(facts, *greens, *((before,) if chained else ()), chol)


def products(at, chol_ref, right_ref, prod_ref):
    def one(p, a):
        i = 4 * a + p
        start = i * DOUBLED - (64 if p % 2 else 0)
        prod_ref[4 * p + a, 0:CHOL, :] = lax.dot_general(
            chol_ref[at, :, start : start + 256], right_ref[p], NT, preferred_element_type=F32
        )

    return [functools.partial(one, p, a) for p in range(4) for a in range(4)]


def crossed(prod_ref, rows, lower, even, totals):
    once, twice = totals
    for a in range(4):
        for b in range(a, 4):
            x = [prod_ref[4 * p + a, rows, b * 128 : b * 128 + 128] for p in range(4)]
            if a == b:
                y = x
            else:
                y = [prod_ref[4 * r + b, rows, a * 128 : a * 128 + 128] for r in range(4)]
            y02 = jnp.where(lower, y[0], y[2])
            y20 = jnp.where(lower, y[2], y[0])
            y13 = jnp.where(lower, y[1], y[3])
            y31 = jnp.where(lower, y[3], y[1])
            z = (
                jnp.where(even, y02, y13),
                jnp.where(even, y13, y02),
                jnp.where(even, y20, y31),
                jnp.where(even, y31, y20),
            )
            part = (x[0] * z[0] + x[1] * z[1]) + (x[2] * z[2] + x[3] * z[3])
            if a == b:
                once = once + part
            else:
                twice = twice + part
    return once, twice


def exchange_kernel(slots, chained, facts_ref, *refs):
    greens, rest = refs[: len(slots)], refs[len(slots) :]
    if chained:
        before_ref, far_ref, out_ref, *scratch = rest
        total = before_ref[...]
    else:
        far_ref, out_ref, *scratch = rest
        total = jnp.zeros((8, 128), F32)
    chol_ref, sems, *scratch = scratch
    right_refs, prod_refs = scratch[:2], scratch[2:]
    copies = [
        pltpu.make_async_copy(far_ref.at[slot], chol_ref.at[at], sems.at[at])
        for at, slot in enumerate(slots)
    ]
    for copy in copies:
        copy.start()
    for copy in copies:
        copy.wait()
    for prod_ref in prod_refs:
        prod_ref[:, ROWS - 8 :, :] = jnp.zeros((16, 8, 512), F32)
    group = lax.broadcasted_iota(jnp.int32, (8, 128), 1) // 32
    lower = group < 2
    even = lax.rem(group, 2) == 0
    zero = jnp.zeros((8, 128), F32)
    chunks = ROWS // 8
    build_right(greens[0][...], right_refs[0])
    for at in range(len(slots) + 1):
        dots = []
        if at < len(slots):
            dots = products(at, chol_ref, right_refs[at % 2], prod_refs[at % 2])
        if at + 1 < len(slots):
            build_right(greens[at + 1][...], right_refs[(at + 1) % 2])
        sums = (zero, zero)
        if not dots:

            def step(k, sums):
                rows = pl.ds(pl.multiple_of(k * 8, 8), 8)
                return crossed(prod_refs[(at + 1) % 2], rows, lower, even, sums)

            sums = lax.fori_loop(0, chunks, step, sums)
        done = 0
        for n, dot in enumerate(dots):
            dot()
            if at:
                upto = (n + 1) * chunks // len(dots)
                for k in range(done, upto):
                    sums = crossed(
                        prod_refs[(at + 1) % 2], slice(8 * k, 8 * k + 8), lower, even, sums
                    )
                done = upto
        if at:
            mult = facts_ref[0:1, slots[at - 1] : slots[at - 1] + 1]
            total = total + mult * (sums[0] + 2.0 * sums[1])
    out_ref[...] = total


def exchange_call(slots, facts, greens, before, chol):
    chained = before is not None
    return pl.pallas_call(
        functools.partial(exchange_kernel, slots, chained),
        out_shape=jax.ShapeDtypeStruct((8, 128), F32),
        in_specs=[VMEM] * (1 + len(slots) + chained)
        + [pl.BlockSpec(memory_space=pl.ANY)],
        out_specs=VMEM,
        scratch_shapes=[
            pltpu.VMEM((len(slots), CHOL, FLAT), BF16),
            pltpu.SemaphoreType.DMA((len(slots),)),
        ]
        + [pltpu.VMEM((4, 512, 256), BF16)] * 2
        + [pltpu.VMEM((16, ROWS, 512), F32)] * 2,
        compiler_params=pltpu.CompilerParams(vmem_limit_bytes=48 * 2**20),
        cost_estimate=pl.CostEstimate(
            flops=len(slots) * 4 * CHOL * 16 * 256 * 512,
            bytes_accessed=len(slots) * CHOL * FLAT * 2,
            transcendentals=0,
        ),
        name="exchange",
    )(facts, *greens, *((before,) if chained else ()), chol)


def share_kernel(got_ref, field_ref, exch_ref, out_ref):
    lane = lax.broadcasted_iota(jnp.int32, (TRANSFERS, 256), 1)
    which = lax.broadcasted_iota(jnp.int32, (128, TRANSFERS), 1).astype(F32)
    more = HALF - 128
    tails = [got_ref[pl.ds(8 + block, 32, stride=ROW_COUNT), :] for block in range(2)]
    rows = []
    for k in range(2 * SLOTS):
        tail = tails[k // 4]
        if k % 4:
            tail = pltpu.roll(tail, 128 - 32 * (k % 4), 1)
        head = got_ref[pl.ds(k, 32, stride=ROW_COUNT), :]
        rows.append(jnp.concatenate([head, tail], 1))
    even = jnp.concatenate(rows[0::2], 0)
    odd = jnp.concatenate(rows[1::2], 0)
    pick = jnp.where(even[:, HALF : HALF + 1] == which, 1.0, 0.0)
    bias = []
    for part in (even, odd):
        total = lax.dot_general(
            pick,
            part,
            (((0,), (0,)), ((), ())),
            precision=lax.Precision.HIGHEST,
            preferred_element_type=F32,
        )
        bias.append(jnp.where(lane < HALF, total, 0.0))
    real, imag = bias
    field = field_ref[...]
    shift_real = STEP * real
    shift_imag = STEP * imag
    terms = (
        0.5 * (real * real - imag * imag),
        field * shift_real - 0.5 * (shift_real * shift_real - shift_imag * shift_imag),
        field * shift_imag - shift_real * shift_imag,
    )
    head = lax.broadcasted_iota(jnp.int32, (1, 128), 1)
    row = jnp.zeros((1, 128), F32)
    for k, term in enumerate(terms):
        row = row + jnp.where(head == 64 + k, jnp.sum(term, keepdims=True), 0.0)
    exch = jnp.sum(exch_ref[...], axis=0, keepdims=True)
    mixed = real[:, 128:] + pltpu.roll(imag[:, 128:], 32, 1) + row
    for ho in range(2):
        for k, line in enumerate((real[:, :128], imag[:, :128], mixed)):
            out_ref[pl.ds(4 * ho + k, 16, stride=8), :] = line
    out_ref[pl.ds(3, 32, stride=4), :] = jnp.broadcast_to(exch, (32, 128))


def share_call(got, field, exch):
    return pl.pallas_call(
        share_kernel,
        out_shape=jax.ShapeDtypeStruct((128, 128), F32),
        compiler_params=pltpu.CompilerParams(vmem_limit_bytes=8 * 2**20),
        name="share",
    )(got, field, exch)


def final_kernel(got_ref, weight_ref, energy_ref, real_ref, imag_ref, pair_ref):
    scalars = got_ref[pl.ds(2, 32, stride=4), :]
    exch = jnp.sum(got_ref[pl.ds(3, 32, stride=4), :], axis=0, keepdims=True)
    exch = jnp.broadcast_to(exch, (8, 128))
    exch = exch + pltpu.roll(exch, 64, 1)
    exch = exch + pltpu.roll(exch, 32, 1)
    exch = exch - pltpu.roll(exch, 128 - WALKERS, 1)
    both = scalars[0:WALKERS] + scalars[WALKERS : 2 * WALKERS]
    lane = lax.broadcasted_iota(jnp.int32, (WALKERS, 128), 1)
    own = lane == lax.broadcasted_iota(jnp.int32, (WALKERS, 128), 0)
    coulomb, real_arg, imag_arg = (
        jnp.sum(jnp.where(own, both[:, k : k + 1], 0.0), axis=0, keepdims=True)
        for k in range(64, 67)
    )
    head = lane[0:1] < WALKERS
    energy = jnp.where(head, coulomb - 0.5 * exch[0:1], 0.0)
    weight = jnp.where(head, weight_ref[...], 0.0)
    top = jnp.sum(weight * energy, keepdims=True)
    bottom = jnp.sum(weight, keepdims=True)
    energy_ref[...] = energy[:, :WALKERS]
    real_ref[...] = real_arg[:, :WALKERS]
    imag_ref[...] = imag_arg[:, :WALKERS]
    pair_ref[...] = jnp.where(lax.broadcasted_iota(jnp.int32, (8, 128), 1) == 0, top, bottom)


def final_call(got, weight):
    return pl.pallas_call(
        final_kernel,
        out_shape=(jax.ShapeDtypeStruct((1, WALKERS), F32),) * 3
        + (jax.ShapeDtypeStruct((8, 128), F32),),
        compiler_params=pltpu.CompilerParams(vmem_limit_bytes=4 * 2**20),
        name="final",
    )(got, weight)


def mixed_kernel(pair_ref, out_ref):
    total = jnp.sum(pair_ref[...], axis=0, keepdims=True)
    out_ref[...] = total[:, 0:1] / total[:, 1:2]


def mixed_call(pair):
    return pl.pallas_call(
        mixed_kernel,
        out_shape=jax.ShapeDtypeStruct((1, 1), F32),
        compiler_params=pltpu.CompilerParams(vmem_limit_bytes=4 * 2**20),
        name="mixed",
    )(pair)


def local(greens, cholesky, slot_source, block_transfer_index, slot_multiplicity, fields, weight):
    parts = lax.axis_size("pb")
    own = lax.axis_index("pb")
    blocks = list(pick_call(slot_source.reshape(1, -1), greens))
    for j in (1, 3, 2):
        offset = offset_of(j, parts)
        pairs = [(d, (d + parts - offset) % parts) for d in range(parts)]
        blocks[j] = lax.ppermute(blocks[j], "pb", pairs)
    half, walker = own // WALKERS, lax.rem(own, WALKERS)
    field = lax.dynamic_index_in_dim(fields, walker, 0, keepdims=False)
    field = lax.dynamic_slice_in_dim(field, half * HALF, HALF, 1)
    field = jnp.pad(field, ((0, 0), (0, 256 - HALF)))

    facts = jnp.concatenate([slot_multiplicity, block_transfer_index]).astype(F32)
    facts = jnp.pad(facts, (0, 128 - 2 * SLOTS)).reshape(1, 128)
    sent = diag_call((0, 1, 2), facts, blocks[:3], None, cholesky)
    sent = diag_call((3,), facts, blocks[3:], sent, cholesky)
    got = lax.all_to_all(sent.reshape(parts, ROW_COUNT, 1, 128), "pb", 0, 0, tiled=True)
    exch = exchange_call((0, 1, 2, 3), facts, blocks, None, cholesky)
    shared = share_call(got.reshape(parts * ROW_COUNT, 128), field, exch)
    final = lax.all_to_all(shared.reshape(parts, 4, 1, 128), "pb", 0, 0, tiled=True)

    wide_weight = jnp.pad(weight, (0, 128 - WALKERS)).reshape(1, 128)
    energy, real_arg, imag_arg, pair = final_call(final.reshape(128, 128), wide_weight)
    pair = lax.all_to_all(pair.reshape(8, 1, 128), "walk", 0, 0, tiled=True)
    mixed = mixed_call(pair.reshape(8, 128)).reshape(())
    mine = lax.dynamic_slice_in_dim(
        final.reshape(parts, 4, 128), lax.rem(own, 2) * WALKERS, WALKERS, 0
    )
    more = HALF - 128
    bias = jnp.stack(
        [jnp.concatenate([mine[:, c], mine[:, 2, 32 * c : 32 * c + more]], 1) for c in range(2)], 1
    )
    energy, real_arg, imag_arg = (x.reshape(WALKERS) for x in (energy, real_arg, imag_arg))
    new_weight = weight * jnp.exp(real_arg) * jnp.maximum(jnp.cos(imag_arg), 0.0)
    return (bias, energy, new_weight, mixed)


def solution(mesh):
    placed = (
        P("walk", "pb", None),
        P("pb", None, None),
        P(),
        P("pb"),
        P("pb"),
        P("walk", None, None),
        P("walk"),
    )
    return jax.shard_map(
        local,
        mesh=mesh,
        in_specs=placed,
        out_specs=(P("walk", None, "pb"), P("walk"), P("walk"), P()),
        check_vma=False,
    )
```

```python
import functools

import jax
import jax.numpy as jnp
from jax import lax
from jax.experimental import pallas as pl
from jax.experimental.pallas import tpu as pltpu
from jax.sharding import PartitionSpec as P

Q_ORB = 96
OCC = 16
CHOL = 300
TRANSFERS = 16
SLOTS = 4
DOUBLED = 2 * Q_ORB
FLAT = OCC * DOUBLED
WALKERS = 16
HALF = CHOL // 2
ROWS = 304
ROW_COUNT = 10
STEP = 0.05
F32 = jnp.float32
BF16 = jnp.bfloat16
NT = (((1,), (1,)), ((), ()))
VMEM = pl.BlockSpec(memory_space=pltpu.VMEM)


def pick_kernel(source_ref, green_ref, *out_refs):
    parts = lax.axis_size("pb")
    own = lax.axis_index("pb")
    lane = lax.broadcasted_iota(jnp.int32, (1, parts * SLOTS), 1)
    source = lax.rem(source_ref[...], 2).astype(F32)
    first = green_ref[:, 0, :].astype(F32)
    second = green_ref[:, 1, :].astype(F32)
    for j, out_ref in enumerate(out_refs):
        reader = lax.rem(own + parts - offset_of(j, parts), parts)
        kpoint = jnp.sum(jnp.where(lane == reader * SLOTS + j, source, 0.0), keepdims=True)
        out_ref[...] = jnp.where(kpoint < 0.5, first, second).astype(BF16)


def offset_of(j, parts):
    return (0, parts - 1, 1, parts // 2)[j]


def pick_call(source, greens):
    return pl.pallas_call(
        pick_kernel,
        out_shape=(jax.ShapeDtypeStruct((WALKERS, FLAT), BF16),) * SLOTS,
        in_specs=[VMEM, VMEM],
        out_specs=(VMEM,) * SLOTS,
        compiler_params=pltpu.CompilerParams(vmem_limit_bytes=4 * 2**20),
        name="pick",
    )(source, greens)


def build_right(green, right_ref):
    window = lax.broadcasted_iota(jnp.int32, (WALKERS, 256), 1)
    for c, plain in enumerate(signed_swapped(green)):
        moved = pltpu.roll(plain, 64, 1)
        for j in range(OCC):
            if j % 2 == 0:
                low = plain[:, j * DOUBLED : j * DOUBLED + 256]
                high = moved[:, j * DOUBLED : j * DOUBLED + 256]
            else:
                high = plain[:, j * DOUBLED - 64 : j * DOUBLED + 192]
                at = j * DOUBLED + 64
                if at + 256 <= FLAT:
                    low = moved[:, at : at + 256]
                else:
                    low = jnp.concatenate([moved[:, at:], moved[:, :128]], 1)
            low = jnp.where(window < DOUBLED, low, 0.0).astype(BF16)
            high = jnp.where(window >= 64, high, 0.0).astype(BF16)
            b, r = divmod(j, 4)
            for p in range(4):
                start = b * 128 + (r ^ p) * 32 + c * 16
                right_ref[p, start : start + 16, :] = low if p % 2 == 0 else high


def signed_swapped(green):
    wide = green.astype(F32)
    lane = lax.broadcasted_iota(jnp.int32, (WALKERS, FLAT), 1)
    first = lax.rem(lane, DOUBLED) < Q_ORB
    swapped = jnp.where(
        first, pltpu.roll(wide, FLAT - Q_ORB, 1), pltpu.roll(wide, Q_ORB, 1)
    )
    signed = jnp.where(first, wide, -wide)
    return signed, swapped


def diag_kernel(slots, chained, facts_ref, *refs):
    greens, rest = refs[: len(slots)], refs[len(slots) :]
    if chained:
        before_ref, chol_ref, out_ref, diag_ref = rest
        out_ref[...] = before_ref[...]
    else:
        chol_ref, out_ref, diag_ref = rest
    diag_ref[CHOL - 4 :, :] = jnp.zeros((512 - CHOL + 4, 128), F32)
    lane = lax.broadcasted_iota(jnp.int32, (16, 128), 1)
    more = HALF - 128
    spill = {}
    for at, slot in enumerate(slots):
        right = jnp.concatenate(signed_swapped(greens[at][...]), 0).astype(BF16)
        diag_ref[0:CHOL, 0:32] = lax.dot_general(
            chol_ref[slot], right, NT, preferred_element_type=F32
        )
        mult = facts_ref[0:1, slot : slot + 1]
        transfer = facts_ref[0:1, SLOTS + slot : SLOTS + slot + 1]
        for h in range(2):
            turned = jnp.transpose(diag_ref[pl.ds(h * HALF, 256), :])
            for c in range(2):
                value = mult * turned[c * 16 : c * 16 + 16, :]
                k = slot * 2 + c
                out_ref[pl.ds(h * 16 * ROW_COUNT + k, 16, stride=ROW_COUNT), :] = value[:, :128]
                tail = jnp.where(
                    lane < more, value[:, 128:], jnp.where(lane == more, transfer, 0.0)
                )
                if k % 4:
                    tail = pltpu.roll(tail, 32 * (k % 4), 1)
                key = (h, k // 4)
                spill[key] = spill[key] + tail if key in spill else tail
    for (h, block), tail in spill.items():
        rows = pl.ds(h * 16 * ROW_COUNT + 8 + block, 16, stride=ROW_COUNT)
        if chained and 2 * block < slots[0]:
            tail = tail + before_ref[rows, :]
        out_ref[rows, :] = tail


def diag_call(slots, facts, greens, before, chol):
    chained = before is not None
    return pl.pallas_call(
        functools.partial(diag_kernel, slots, chained),
        out_shape=jax.ShapeDtypeStruct((32 * ROW_COUNT, 128), F32),
        in_specs=[VMEM] * (2 + len(slots) + chained),
        out_specs=VMEM,
        scratch_shapes=[pltpu.VMEM((512, 128), F32)],
        compiler_params=pltpu.CompilerParams(vmem_limit_bytes=8 * 2**20),
        cost_estimate=pl.CostEstimate(
            flops=len(slots) * 2 * CHOL * FLAT * 256,
            bytes_accessed=len(slots) * CHOL * FLAT * 2,
            transcendentals=0,
        ),
        name="diag",
    )(facts, *greens, *((before,) if chained else ()), chol)


def products(at, chol_ref, right_ref, prod_ref):
    def one(p, a):
        i = 4 * a + p
        start = i * DOUBLED - (64 if p % 2 else 0)
        prod_ref[4 * p + a, 0:CHOL, :] = lax.dot_general(
            chol_ref[at, :, start : start + 256], right_ref[p], NT, preferred_element_type=F32
        )

    return [functools.partial(one, p, a) for p in range(4) for a in range(4)]


def crossed(prod_ref, rows, lower, even, totals):
    once, twice = totals
    for a in range(4):
        for b in range(a, 4):
            x = [prod_ref[4 * p + a, rows, b * 128 : b * 128 + 128] for p in range(4)]
            if a == b:
                y = x
            else:
                y = [prod_ref[4 * r + b, rows, a * 128 : a * 128 + 128] for r in range(4)]
            y02 = jnp.where(lower, y[0], y[2])
            y20 = jnp.where(lower, y[2], y[0])
            y13 = jnp.where(lower, y[1], y[3])
            y31 = jnp.where(lower, y[3], y[1])
            z = (
                jnp.where(even, y02, y13),
                jnp.where(even, y13, y02),
                jnp.where(even, y20, y31),
                jnp.where(even, y31, y20),
            )
            part = (x[0] * z[0] + x[1] * z[1]) + (x[2] * z[2] + x[3] * z[3])
            if a == b:
                once = once + part
            else:
                twice = twice + part
    return once, twice


def exchange_kernel(slots, chained, facts_ref, *refs):
    greens, rest = refs[: len(slots)], refs[len(slots) :]
    if chained:
        before_ref, far_ref, out_ref, *scratch = rest
        total = before_ref[...]
    else:
        far_ref, out_ref, *scratch = rest
        total = jnp.zeros((8, 128), F32)
    chol_ref, sems, *scratch = scratch
    right_refs, prod_refs = scratch[:2], scratch[2:]
    copies = [
        pltpu.make_async_copy(far_ref.at[slot], chol_ref.at[at], sems.at[at])
        for at, slot in enumerate(slots)
    ]
    for copy in copies:
        copy.start()
    for copy in copies:
        copy.wait()
    for prod_ref in prod_refs:
        prod_ref[:, ROWS - 8 :, :] = jnp.zeros((16, 8, 512), F32)
    group = lax.broadcasted_iota(jnp.int32, (8, 128), 1) // 32
    lower = group < 2
    even = lax.rem(group, 2) == 0
    zero = jnp.zeros((8, 128), F32)
    chunks = ROWS // 8
    build_right(greens[0][...], right_refs[0])
    for at in range(len(slots) + 1):
        dots = []
        if at < len(slots):
            dots = products(at, chol_ref, right_refs[at % 2], prod_refs[at % 2])
        if at + 1 < len(slots):
            build_right(greens[at + 1][...], right_refs[(at + 1) % 2])
        sums = (zero, zero)
        if not dots:

            def step(k, sums):
                rows = pl.ds(pl.multiple_of(k * 8, 8), 8)
                return crossed(prod_refs[(at + 1) % 2], rows, lower, even, sums)

            sums = lax.fori_loop(0, chunks, step, sums, unroll=38)
        done = 0
        for n, dot in enumerate(dots):
            dot()
            if at:
                upto = (n + 1) * chunks // len(dots)
                for k in range(done, upto):
                    sums = crossed(
                        prod_refs[(at + 1) % 2], slice(8 * k, 8 * k + 8), lower, even, sums
                    )
                done = upto
        if at:
            mult = facts_ref[0:1, slots[at - 1] : slots[at - 1] + 1]
            total = total + mult * (sums[0] + 2.0 * sums[1])
    out_ref[...] = total


def exchange_call(slots, facts, greens, before, chol):
    chained = before is not None
    return pl.pallas_call(
        functools.partial(exchange_kernel, slots, chained),
        out_shape=jax.ShapeDtypeStruct((8, 128), F32),
        in_specs=[VMEM] * (1 + len(slots) + chained)
        + [pl.BlockSpec(memory_space=pl.ANY)],
        out_specs=VMEM,
        scratch_shapes=[
            pltpu.VMEM((len(slots), CHOL, FLAT), BF16),
            pltpu.SemaphoreType.DMA((len(slots),)),
        ]
        + [pltpu.VMEM((4, 512, 256), BF16)] * 2
        + [pltpu.VMEM((16, ROWS, 512), F32)] * 2,
        compiler_params=pltpu.CompilerParams(vmem_limit_bytes=48 * 2**20),
        cost_estimate=pl.CostEstimate(
            flops=len(slots) * 4 * CHOL * 16 * 256 * 512,
            bytes_accessed=len(slots) * CHOL * FLAT * 2,
            transcendentals=0,
        ),
        name="exchange",
    )(facts, *greens, *((before,) if chained else ()), chol)


def share_kernel(got_ref, field_ref, exch_ref, out_ref):
    lane = lax.broadcasted_iota(jnp.int32, (TRANSFERS, 256), 1)
    which = lax.broadcasted_iota(jnp.int32, (128, TRANSFERS), 1).astype(F32)
    more = HALF - 128
    tails = [got_ref[pl.ds(8 + block, 32, stride=ROW_COUNT), :] for block in range(2)]
    rows = []
    for k in range(2 * SLOTS):
        tail = tails[k // 4]
        if k % 4:
            tail = pltpu.roll(tail, 128 - 32 * (k % 4), 1)
        head = got_ref[pl.ds(k, 32, stride=ROW_COUNT), :]
        rows.append(jnp.concatenate([head, tail], 1))
    even = jnp.concatenate(rows[0::2], 0)
    odd = jnp.concatenate(rows[1::2], 0)
    pick = jnp.where(even[:, HALF : HALF + 1] == which, 1.0, 0.0)
    bias = []
    for part in (even, odd):
        total = lax.dot_general(
            pick,
            part,
            (((0,), (0,)), ((), ())),
            precision=lax.Precision.HIGHEST,
            preferred_element_type=F32,
        )
        bias.append(jnp.where(lane < HALF, total, 0.0))
    real, imag = bias
    field = field_ref[...]
    shift_real = STEP * real
    shift_imag = STEP * imag
    terms = (
        0.5 * (real * real - imag * imag),
        field * shift_real - 0.5 * (shift_real * shift_real - shift_imag * shift_imag),
        field * shift_imag - shift_real * shift_imag,
    )
    head = lax.broadcasted_iota(jnp.int32, (1, 128), 1)
    row = jnp.zeros((1, 128), F32)
    for k, term in enumerate(terms):
        row = row + jnp.where(head == 64 + k, jnp.sum(term, keepdims=True), 0.0)
    exch = jnp.sum(exch_ref[...], axis=0, keepdims=True)
    mixed = real[:, 128:] + pltpu.roll(imag[:, 128:], 32, 1) + row
    for ho in range(2):
        for k, line in enumerate((real[:, :128], imag[:, :128], mixed)):
            out_ref[pl.ds(4 * ho + k, 16, stride=8), :] = line
    out_ref[pl.ds(3, 32, stride=4), :] = jnp.broadcast_to(exch, (32, 128))


def share_call(got, field, exch):
    return pl.pallas_call(
        share_kernel,
        out_shape=jax.ShapeDtypeStruct((128, 128), F32),
        compiler_params=pltpu.CompilerParams(vmem_limit_bytes=8 * 2**20),
        name="share",
    )(got, field, exch)


def final_kernel(got_ref, weight_ref, energy_ref, real_ref, imag_ref, pair_ref):
    scalars = got_ref[pl.ds(2, 32, stride=4), :]
    exch = jnp.sum(got_ref[pl.ds(3, 32, stride=4), :], axis=0, keepdims=True)
    exch = jnp.broadcast_to(exch, (8, 128))
    exch = exch + pltpu.roll(exch, 64, 1)
    exch = exch + pltpu.roll(exch, 32, 1)
    exch = exch - pltpu.roll(exch, 128 - WALKERS, 1)
    both = scalars[0:WALKERS] + scalars[WALKERS : 2 * WALKERS]
    lane = lax.broadcasted_iota(jnp.int32, (WALKERS, 128), 1)
    own = lane == lax.broadcasted_iota(jnp.int32, (WALKERS, 128), 0)
    coulomb, real_arg, imag_arg = (
        jnp.sum(jnp.where(own, both[:, k : k + 1], 0.0), axis=0, keepdims=True)
        for k in range(64, 67)
    )
    head = lane[0:1] < WALKERS
    energy = jnp.where(head, coulomb - 0.5 * exch[0:1], 0.0)
    weight = jnp.where(head, weight_ref[...], 0.0)
    top = jnp.sum(weight * energy, keepdims=True)
    bottom = jnp.sum(weight, keepdims=True)
    energy_ref[...] = energy[:, :WALKERS]
    real_ref[...] = real_arg[:, :WALKERS]
    imag_ref[...] = imag_arg[:, :WALKERS]
    pair_ref[...] = jnp.where(lax.broadcasted_iota(jnp.int32, (8, 128), 1) == 0, top, bottom)


def final_call(got, weight):
    return pl.pallas_call(
        final_kernel,
        out_shape=(jax.ShapeDtypeStruct((1, WALKERS), F32),) * 3
        + (jax.ShapeDtypeStruct((8, 128), F32),),
        compiler_params=pltpu.CompilerParams(vmem_limit_bytes=4 * 2**20),
        name="final",
    )(got, weight)


def mixed_kernel(pair_ref, out_ref):
    total = jnp.sum(pair_ref[...], axis=0, keepdims=True)
    out_ref[...] = total[:, 0:1] / total[:, 1:2]


def mixed_call(pair):
    return pl.pallas_call(
        mixed_kernel,
        out_shape=jax.ShapeDtypeStruct((1, 1), F32),
        compiler_params=pltpu.CompilerParams(vmem_limit_bytes=4 * 2**20),
        name="mixed",
    )(pair)


def local(greens, cholesky, slot_source, block_transfer_index, slot_multiplicity, fields, weight):
    parts = lax.axis_size("pb")
    own = lax.axis_index("pb")
    blocks = list(pick_call(slot_source.reshape(1, -1), greens))
    for j in (1, 3, 2):
        offset = offset_of(j, parts)
        pairs = [(d, (d + parts - offset) % parts) for d in range(parts)]
        blocks[j] = lax.ppermute(blocks[j], "pb", pairs)
    half, walker = own // WALKERS, lax.rem(own, WALKERS)
    field = lax.dynamic_index_in_dim(fields, walker, 0, keepdims=False)
    field = lax.dynamic_slice_in_dim(field, half * HALF, HALF, 1)
    field = jnp.pad(field, ((0, 0), (0, 256 - HALF)))

    facts = jnp.concatenate([slot_multiplicity, block_transfer_index]).astype(F32)
    facts = jnp.pad(facts, (0, 128 - 2 * SLOTS)).reshape(1, 128)
    sent = diag_call((0,), facts, blocks[:1], None, cholesky)
    sent = diag_call((1, 2, 3), facts, blocks[1:], sent, cholesky)
    got = lax.all_to_all(sent.reshape(parts, ROW_COUNT, 1, 128), "pb", 0, 0, tiled=True)
    exch = exchange_call((0, 1, 2, 3), facts, blocks, None, cholesky)
    shared = share_call(got.reshape(parts * ROW_COUNT, 128), field, exch)
    final = lax.all_to_all(shared.reshape(parts, 4, 1, 128), "pb", 0, 0, tiled=True)

    wide_weight = jnp.pad(weight, (0, 128 - WALKERS)).reshape(1, 128)
    energy, real_arg, imag_arg, pair = final_call(final.reshape(128, 128), wide_weight)
    pair = lax.all_to_all(pair.reshape(8, 1, 128), "walk", 0, 0, tiled=True)
    mixed = mixed_call(pair.reshape(8, 128)).reshape(())
    mine = lax.dynamic_slice_in_dim(
        final.reshape(parts, 4, 128), lax.rem(own, 2) * WALKERS, WALKERS, 0
    )
    more = HALF - 128
    bias = jnp.stack(
        [jnp.concatenate([mine[:, c], mine[:, 2, 32 * c : 32 * c + more]], 1) for c in range(2)], 1
    )
    energy, real_arg, imag_arg = (x.reshape(WALKERS) for x in (energy, real_arg, imag_arg))
    new_weight = weight * jnp.exp(real_arg) * jnp.maximum(jnp.cos(imag_arg), 0.0)
    return (bias, energy, new_weight, mixed)


def solution(mesh):
    placed = (
        P("walk", "pb", None),
        P("pb", None, None),
        P(),
        P("pb"),
        P("pb"),
        P("walk", None, None),
        P("walk"),
    )
    return jax.shard_map(
        local,
        mesh=mesh,
        in_specs=placed,
        out_specs=(P("walk", None, "pb"), P("walk"), P("walk"), P()),
        check_vma=False,
    )
```

```python
import functools

import jax
import jax.numpy as jnp
from jax import lax
from jax.experimental import pallas as pl
from jax.experimental.pallas import tpu as pltpu
from jax.sharding import PartitionSpec as P

Q_ORB = 96
OCC = 16
CHOL = 300
TRANSFERS = 16
SLOTS = 4
DOUBLED = 2 * Q_ORB
FLAT = OCC * DOUBLED
WALKERS = 16
HALF = CHOL // 2
ROWS = 304
ROW_COUNT = 10
LANE_CUTS = 2
STEP = 0.05
F32 = jnp.float32
BF16 = jnp.bfloat16
NT = (((1,), (1,)), ((), ()))
VMEM = pl.BlockSpec(memory_space=pltpu.VMEM)


def pick_kernel(source_ref, green_ref, *out_refs):
    parts = lax.axis_size("pb")
    own = lax.axis_index("pb")
    lane = lax.broadcasted_iota(jnp.int32, (1, parts * SLOTS), 1)
    source = lax.rem(source_ref[...], 2).astype(F32)
    first = green_ref[:, 0, :].astype(F32)
    second = green_ref[:, 1, :].astype(F32)
    for j, out_ref in enumerate(out_refs):
        reader = lax.rem(own + parts - offset_of(j, parts), parts)
        kpoint = jnp.sum(jnp.where(lane == reader * SLOTS + j, source, 0.0), keepdims=True)
        out_ref[...] = jnp.where(kpoint < 0.5, first, second).astype(BF16)


def offset_of(j, parts):
    return (0, parts - 1, 1, parts // 2)[j]


def pick_call(source, greens):
    return pl.pallas_call(
        pick_kernel,
        out_shape=(jax.ShapeDtypeStruct((WALKERS, FLAT), BF16),) * SLOTS,
        in_specs=[VMEM, VMEM],
        out_specs=(VMEM,) * SLOTS,
        compiler_params=pltpu.CompilerParams(vmem_limit_bytes=4 * 2**20),
        name="pick",
    )(source, greens)


def build_right(green, right_ref):
    window = lax.broadcasted_iota(jnp.int32, (WALKERS, 256), 1)
    for c, plain in enumerate(signed_swapped(green)):
        moved = pltpu.roll(plain, 64, 1)
        for j in range(OCC):
            if j % 2 == 0:
                low = plain[:, j * DOUBLED : j * DOUBLED + 256]
                high = moved[:, j * DOUBLED : j * DOUBLED + 256]
            else:
                high = plain[:, j * DOUBLED - 64 : j * DOUBLED + 192]
                at = j * DOUBLED + 64
                if at + 256 <= FLAT:
                    low = moved[:, at : at + 256]
                else:
                    low = jnp.concatenate([moved[:, at:], moved[:, :128]], 1)
            low = jnp.where(window < DOUBLED, low, 0.0).astype(BF16)
            high = jnp.where(window >= 64, high, 0.0).astype(BF16)
            b, r = divmod(j, 4)
            for p in range(4):
                start = b * 128 + (r ^ p) * 32 + c * 16
                right_ref[p, start : start + 16, :] = low if p % 2 == 0 else high


def signed_swapped(green):
    wide = green.astype(F32)
    lane = lax.broadcasted_iota(jnp.int32, (WALKERS, FLAT), 1)
    first = lax.rem(lane, DOUBLED) < Q_ORB
    swapped = jnp.where(
        first, pltpu.roll(wide, FLAT - Q_ORB, 1), pltpu.roll(wide, Q_ORB, 1)
    )
    signed = jnp.where(first, wide, -wide)
    return signed, swapped


def diag_kernel(slots, chained, facts_ref, *refs):
    greens, rest = refs[: len(slots)], refs[len(slots) :]
    if chained:
        before_ref, chol_ref, out_ref, diag_ref = rest
        out_ref[...] = before_ref[...]
    else:
        chol_ref, out_ref, diag_ref = rest
    diag_ref[CHOL - 4 :, :] = jnp.zeros((512 - CHOL + 4, 128), F32)
    lane = lax.broadcasted_iota(jnp.int32, (16, 128), 1)
    more = HALF - 128
    spill = {}
    for at, slot in enumerate(slots):
        right = jnp.concatenate(signed_swapped(greens[at][...]), 0).astype(BF16)
        diag_ref[0:CHOL, 0:32] = lax.dot_general(
            chol_ref[slot], right, NT, preferred_element_type=F32
        )
        mult = facts_ref[0:1, slot : slot + 1]
        transfer = facts_ref[0:1, SLOTS + slot : SLOTS + slot + 1]
        for h in range(2):
            turned = jnp.transpose(diag_ref[pl.ds(h * HALF, 256), :])
            for c in range(2):
                value = mult * turned[c * 16 : c * 16 + 16, :]
                k = slot * 2 + c
                out_ref[pl.ds(h * 16 * ROW_COUNT + k, 16, stride=ROW_COUNT), :] = value[:, :128]
                tail = jnp.where(
                    lane < more, value[:, 128:], jnp.where(lane == more, transfer, 0.0)
                )
                if k % 4:
                    tail = pltpu.roll(tail, 32 * (k % 4), 1)
                key = (h, k // 4)
                spill[key] = spill[key] + tail if key in spill else tail
    for (h, block), tail in spill.items():
        rows = pl.ds(h * 16 * ROW_COUNT + 8 + block, 16, stride=ROW_COUNT)
        if chained and 2 * block < slots[0]:
            tail = tail + before_ref[rows, :]
        out_ref[rows, :] = tail


def diag_call(slots, facts, greens, before, chol):
    chained = before is not None
    return pl.pallas_call(
        functools.partial(diag_kernel, slots, chained),
        out_shape=jax.ShapeDtypeStruct((32 * ROW_COUNT, 128), F32),
        in_specs=[VMEM] * (2 + len(slots) + chained),
        out_specs=VMEM,
        scratch_shapes=[pltpu.VMEM((512, 128), F32)],
        compiler_params=pltpu.CompilerParams(vmem_limit_bytes=8 * 2**20),
        cost_estimate=pl.CostEstimate(
            flops=len(slots) * 2 * CHOL * FLAT * 256,
            bytes_accessed=len(slots) * CHOL * FLAT * 2,
            transcendentals=0,
        ),
        name="diag",
    )(facts, *greens, *((before,) if chained else ()), chol)


def products(at, chol_ref, right_ref, prod_ref):
    def one(p, a):
        i = 4 * a + p
        start = i * DOUBLED - (64 if p % 2 else 0)
        prod_ref[4 * p + a, 0:CHOL, :] = lax.dot_general(
            chol_ref[at, :, start : start + 256], right_ref[p], NT, preferred_element_type=F32
        )

    return [functools.partial(one, p, a) for p in range(4) for a in range(4)]


def crossed(prod_ref, rows, lower, even, totals):
    once, twice = totals
    for a in range(4):
        for b in range(a, 4):
            x = [prod_ref[4 * p + a, rows, b * 128 : b * 128 + 128] for p in range(4)]
            if a == b:
                y = x
            else:
                y = [prod_ref[4 * r + b, rows, a * 128 : a * 128 + 128] for r in range(4)]
            y02 = jnp.where(lower, y[0], y[2])
            y20 = jnp.where(lower, y[2], y[0])
            y13 = jnp.where(lower, y[1], y[3])
            y31 = jnp.where(lower, y[3], y[1])
            z = (
                jnp.where(even, y02, y13),
                jnp.where(even, y13, y02),
                jnp.where(even, y20, y31),
                jnp.where(even, y31, y20),
            )
            part = (x[0] * z[0] + x[1] * z[1]) + (x[2] * z[2] + x[3] * z[3])
            if a == b:
                once = once + part
            else:
                twice = twice + part
    return once, twice


def exchange_kernel(slots, chained, facts_ref, *refs):
    greens, rest = refs[: len(slots)], refs[len(slots) :]
    if chained:
        before_ref, far_ref, out_ref, *scratch = rest
        total = before_ref[...]
    else:
        far_ref, out_ref, *scratch = rest
        total = jnp.zeros((8, 128), F32)
    chol_ref, sems, *scratch = scratch
    right_refs, prod_refs = scratch[:2], scratch[2:]
    width = FLAT // LANE_CUTS
    copies = [
        pltpu.make_async_copy(
            far_ref.at[slot, :, cut * width : (cut + 1) * width],
            chol_ref.at[at, :, cut * width : (cut + 1) * width],
            sems.at[at, cut],
        )
        for at, slot in enumerate(slots)
        for cut in range(LANE_CUTS)
    ]
    for copy in copies:
        copy.start()
    for copy in copies:
        copy.wait()
    for prod_ref in prod_refs:
        prod_ref[:, ROWS - 8 :, :] = jnp.zeros((16, 8, 512), F32)
    group = lax.broadcasted_iota(jnp.int32, (8, 128), 1) // 32
    lower = group < 2
    even = lax.rem(group, 2) == 0
    zero = jnp.zeros((8, 128), F32)
    chunks = ROWS // 8
    build_right(greens[0][...], right_refs[0])
    for at in range(len(slots) + 1):
        dots = []
        if at < len(slots):
            dots = products(at, chol_ref, right_refs[at % 2], prod_refs[at % 2])
        if at + 1 < len(slots):
            build_right(greens[at + 1][...], right_refs[(at + 1) % 2])
        sums = (zero, zero)
        if not dots:

            def step(k, sums):
                rows = pl.ds(pl.multiple_of(k * 8, 8), 8)
                return crossed(prod_refs[(at + 1) % 2], rows, lower, even, sums)

            sums = lax.fori_loop(0, chunks, step, sums, unroll=38)
        done = 0
        for n, dot in enumerate(dots):
            dot()
            if at:
                upto = (n + 1) * chunks // len(dots)
                for k in range(done, upto):
                    sums = crossed(
                        prod_refs[(at + 1) % 2], slice(8 * k, 8 * k + 8), lower, even, sums
                    )
                done = upto
        if at:
            mult = facts_ref[0:1, slots[at - 1] : slots[at - 1] + 1]
            total = total + mult * (sums[0] + 2.0 * sums[1])
    out_ref[...] = total


def exchange_call(slots, facts, greens, before, chol):
    chained = before is not None
    return pl.pallas_call(
        functools.partial(exchange_kernel, slots, chained),
        out_shape=jax.ShapeDtypeStruct((8, 128), F32),
        in_specs=[VMEM] * (1 + len(slots) + chained)
        + [pl.BlockSpec(memory_space=pl.ANY)],
        out_specs=VMEM,
        scratch_shapes=[
            pltpu.VMEM((len(slots), CHOL, FLAT), BF16),
            pltpu.SemaphoreType.DMA((len(slots), LANE_CUTS)),
        ]
        + [pltpu.VMEM((4, 512, 256), BF16)] * 2
        + [pltpu.VMEM((16, ROWS, 512), F32)] * 2,
        compiler_params=pltpu.CompilerParams(vmem_limit_bytes=48 * 2**20),
        cost_estimate=pl.CostEstimate(
            flops=len(slots) * 4 * CHOL * 16 * 256 * 512,
            bytes_accessed=len(slots) * CHOL * FLAT * 2,
            transcendentals=0,
        ),
        name="exchange",
    )(facts, *greens, *((before,) if chained else ()), chol)


def share_kernel(got_ref, field_ref, exch_ref, out_ref):
    lane = lax.broadcasted_iota(jnp.int32, (TRANSFERS, 256), 1)
    which = lax.broadcasted_iota(jnp.int32, (128, TRANSFERS), 1).astype(F32)
    more = HALF - 128
    tails = [got_ref[pl.ds(8 + block, 32, stride=ROW_COUNT), :] for block in range(2)]
    rows = []
    for k in range(2 * SLOTS):
        tail = tails[k // 4]
        if k % 4:
            tail = pltpu.roll(tail, 128 - 32 * (k % 4), 1)
        head = got_ref[pl.ds(k, 32, stride=ROW_COUNT), :]
        rows.append(jnp.concatenate([head, tail], 1))
    even = jnp.concatenate(rows[0::2], 0)
    odd = jnp.concatenate(rows[1::2], 0)
    pick = jnp.where(even[:, HALF : HALF + 1] == which, 1.0, 0.0)
    bias = []
    for part in (even, odd):
        total = lax.dot_general(
            pick,
            part,
            (((0,), (0,)), ((), ())),
            precision=lax.Precision.HIGHEST,
            preferred_element_type=F32,
        )
        bias.append(jnp.where(lane < HALF, total, 0.0))
    real, imag = bias
    field = field_ref[...]
    shift_real = STEP * real
    shift_imag = STEP * imag
    terms = (
        0.5 * (real * real - imag * imag),
        field * shift_real - 0.5 * (shift_real * shift_real - shift_imag * shift_imag),
        field * shift_imag - shift_real * shift_imag,
    )
    head = lax.broadcasted_iota(jnp.int32, (1, 128), 1)
    row = jnp.zeros((1, 128), F32)
    for k, term in enumerate(terms):
        row = row + jnp.where(head == 64 + k, jnp.sum(term, keepdims=True), 0.0)
    exch = jnp.sum(exch_ref[...], axis=0, keepdims=True)
    mixed = real[:, 128:] + pltpu.roll(imag[:, 128:], 32, 1) + row
    for ho in range(2):
        for k, line in enumerate((real[:, :128], imag[:, :128], mixed)):
            out_ref[pl.ds(4 * ho + k, 16, stride=8), :] = line
    out_ref[pl.ds(3, 32, stride=4), :] = jnp.broadcast_to(exch, (32, 128))


def share_call(got, field, exch):
    return pl.pallas_call(
        share_kernel,
        out_shape=jax.ShapeDtypeStruct((128, 128), F32),
        compiler_params=pltpu.CompilerParams(vmem_limit_bytes=8 * 2**20),
        name="share",
    )(got, field, exch)


def final_kernel(got_ref, weight_ref, energy_ref, real_ref, imag_ref, pair_ref):
    scalars = got_ref[pl.ds(2, 32, stride=4), :]
    exch = jnp.sum(got_ref[pl.ds(3, 32, stride=4), :], axis=0, keepdims=True)
    exch = jnp.broadcast_to(exch, (8, 128))
    exch = exch + pltpu.roll(exch, 64, 1)
    exch = exch + pltpu.roll(exch, 32, 1)
    exch = exch - pltpu.roll(exch, 128 - WALKERS, 1)
    both = scalars[0:WALKERS] + scalars[WALKERS : 2 * WALKERS]
    lane = lax.broadcasted_iota(jnp.int32, (WALKERS, 128), 1)
    own = lane == lax.broadcasted_iota(jnp.int32, (WALKERS, 128), 0)
    coulomb, real_arg, imag_arg = (
        jnp.sum(jnp.where(own, both[:, k : k + 1], 0.0), axis=0, keepdims=True)
        for k in range(64, 67)
    )
    head = lane[0:1] < WALKERS
    energy = jnp.where(head, coulomb - 0.5 * exch[0:1], 0.0)
    weight = jnp.where(head, weight_ref[...], 0.0)
    top = jnp.sum(weight * energy, keepdims=True)
    bottom = jnp.sum(weight, keepdims=True)
    energy_ref[...] = energy[:, :WALKERS]
    real_ref[...] = real_arg[:, :WALKERS]
    imag_ref[...] = imag_arg[:, :WALKERS]
    pair_ref[...] = jnp.where(lax.broadcasted_iota(jnp.int32, (8, 128), 1) == 0, top, bottom)


def final_call(got, weight):
    return pl.pallas_call(
        final_kernel,
        out_shape=(jax.ShapeDtypeStruct((1, WALKERS), F32),) * 3
        + (jax.ShapeDtypeStruct((8, 128), F32),),
        compiler_params=pltpu.CompilerParams(vmem_limit_bytes=4 * 2**20),
        name="final",
    )(got, weight)


def mixed_kernel(pair_ref, out_ref):
    total = jnp.sum(pair_ref[...], axis=0, keepdims=True)
    out_ref[...] = total[:, 0:1] / total[:, 1:2]


def mixed_call(pair):
    return pl.pallas_call(
        mixed_kernel,
        out_shape=jax.ShapeDtypeStruct((1, 1), F32),
        compiler_params=pltpu.CompilerParams(vmem_limit_bytes=4 * 2**20),
        name="mixed",
    )(pair)


def local(greens, cholesky, slot_source, block_transfer_index, slot_multiplicity, fields, weight):
    parts = lax.axis_size("pb")
    own = lax.axis_index("pb")
    blocks = list(pick_call(slot_source.reshape(1, -1), greens))
    for j in (1, 3, 2):
        offset = offset_of(j, parts)
        pairs = [(d, (d + parts - offset) % parts) for d in range(parts)]
        blocks[j] = lax.ppermute(blocks[j], "pb", pairs)
    half, walker = own // WALKERS, lax.rem(own, WALKERS)
    field = lax.dynamic_index_in_dim(fields, walker, 0, keepdims=False)
    field = lax.dynamic_slice_in_dim(field, half * HALF, HALF, 1)
    field = jnp.pad(field, ((0, 0), (0, 256 - HALF)))

    facts = jnp.concatenate([slot_multiplicity, block_transfer_index]).astype(F32)
    facts = jnp.pad(facts, (0, 128 - 2 * SLOTS)).reshape(1, 128)
    sent = diag_call((0,), facts, blocks[:1], None, cholesky)
    sent = diag_call((1, 2, 3), facts, blocks[1:], sent, cholesky)
    got = lax.all_to_all(sent.reshape(parts, ROW_COUNT, 1, 128), "pb", 0, 0, tiled=True)
    exch = exchange_call((0, 1, 2, 3), facts, blocks, None, cholesky)
    shared = share_call(got.reshape(parts * ROW_COUNT, 128), field, exch)
    final = lax.all_to_all(shared.reshape(parts, 4, 1, 128), "pb", 0, 0, tiled=True)

    wide_weight = jnp.pad(weight, (0, 128 - WALKERS)).reshape(1, 128)
    energy, real_arg, imag_arg, pair = final_call(final.reshape(128, 128), wide_weight)
    pair = lax.all_to_all(pair.reshape(8, 1, 128), "walk", 0, 0, tiled=True)
    mixed = mixed_call(pair.reshape(8, 128)).reshape(())
    mine = lax.dynamic_slice_in_dim(
        final.reshape(parts, 4, 128), lax.rem(own, 2) * WALKERS, WALKERS, 0
    )
    more = HALF - 128
    bias = jnp.stack(
        [jnp.concatenate([mine[:, c], mine[:, 2, 32 * c : 32 * c + more]], 1) for c in range(2)], 1
    )
    energy, real_arg, imag_arg = (x.reshape(WALKERS) for x in (energy, real_arg, imag_arg))
    new_weight = weight * jnp.exp(real_arg) * jnp.maximum(jnp.cos(imag_arg), 0.0)
    return (bias, energy, new_weight, mixed)


def solution(mesh):
    placed = (
        P("walk", "pb", None),
        P("pb", None, None),
        P(),
        P("pb"),
        P("pb"),
        P("walk", None, None),
        P("walk"),
    )
    return jax.shard_map(
        local,
        mesh=mesh,
        in_specs=placed,
        out_specs=(P("walk", None, "pb"), P("walk"), P("walk"), P()),
        check_vma=False,
    )
```
